512 devices in a mesh: col: 32 (over z, core), row: 16 (over y, x).
Axes of the slice: x: 4, y: 4, z: 16, core: 2. Of those that a mesh axis runs over, the one named last changes fastest.
Arguments:
- panel: bfloat16 [32, 512, 1024], P('row', 'col'), may hold values from -2.5 to 2.5
- dblocks: bfloat16 [2, 512, 512], replicated, may hold values from -4 to 4, as said below
- dense_tiles: bfloat16 [16384, 16384], P('row', 'col'), may hold values from -6 to 6
- left_factor: bfloat16 [32, 64, 16384], P('col', None, 'row'), may hold values from -0.75 to 0.75
- right_factor: bfloat16 [32, 64, 16384], P('row', None, 'col'), may hold values from -6 to 6
- sketch: bfloat16 [64, 16384], P(None, 'col'), may hold values from -0.25 to 0.25
- pattern: int32 [32, 32], replicated, may hold values 0 or 1
- colmap: int32 [32], replicated, may hold values from 0 to 31, each once
Outputs:
- dense_out: bfloat16 [16384, 16384], P('row', 'col')
- sketch_out: bfloat16 [32, 64, 16384], P('col', None, 'row')
The draws below stay inside these ranges and needn't reach their ends.
Inputs may be any that keep to these rules, and one draw needn't show every extreme that they name: `dblocks`: each of the 2 blocks is symmetric. `colmap`: every panel tile appears once.
All inputs are finite; a program needn't handle non-finite values.
Results may differ from the reference program's by a relative error of at most 0.0055.
Values may be sent and summed in bfloat16 or wider, within the bound.
No kernel may reach another device: no remote copies, remote signals or barrier semaphores. Data moves between devices by JAX's collectives and lax.ppermute only.
A program may use at most 64 MiB of HBM per device.

```python
import math
import jax
import jax.numpy as jnp
from jax import lax

B = 512
K = 64
PT = 2
PW = 1024
NT = 32
N = 16384


def draw_dblocks(key, part):
    key = jax.random.fold_in(key, 7)
    key_sym, key_mag, key_sign = jax.random.split(key, 3)
    base = jax.random.normal(key_sym, (PT, B, B), jnp.float32)
    symmetric = (base + jnp.swapaxes(base, 1, 2)) * (0.5 / math.sqrt(B))
    magnitude = jnp.exp(jax.random.uniform(key_mag, (PT, B), jnp.float32, math.log(0.5), math.log(2.0)))
    signs = jnp.where(jax.random.bernoulli(key_sign, 0.5, (PT, B)), 1.0, -1.0)
    identity = jnp.eye(B, dtype=jnp.float32)
    result = symmetric + identity[None, :, :] * (signs * magnitude)[:, :, None]
    return jnp.clip(result, -4.0, 4.0).astype(jnp.bfloat16)


def touch_ends(array, rng, low, top_value):
    longest = array.shape.index(max(array.shape))
    spots = []
    for shift in (0, 1):
        where = [jax.random.randint(jax.random.fold_in(rng, axis), (), 0, length) for axis, length in enumerate(array.shape)]
        where[longest] = (where[longest] + shift) % array.shape[longest]
        spots.append(tuple(where))
    return array.at[spots[0]].set(low).at[spots[1]].set(top_value)


def block_levels(key, shape, pieces, low, top_value):
    gain = 1.0
    for axis_at, parts in pieces:
        heights = jax.random.uniform(jax.random.fold_in(jax.random.fold_in(key, 6), axis_at), (parts,), jnp.float32, low / len(pieces), top_value / len(pieces))
        gain = gain * jnp.repeat(jnp.exp(heights), shape[axis_at] // parts).reshape((-1,) + (1,) * (len(shape) - 1 - axis_at))
    return gain


def bell_draw(key, extent, deviation, most, shards=(), kind=jnp.bfloat16):
    values = deviation * jax.random.normal(key, extent, jnp.float32)
    if shards:
        values = values * block_levels(key, extent, shards, -0.22, 0.18)
    return jnp.clip(values, -most, most).astype(kind)


def setup_inputs(seed: int = 0) -> dict:
    splits = jax.random.split(jax.random.key(seed), 9)
    return {
        "panel": bell_draw(splits[0], (NT, B, PW), (1.0 * PW ** -0.25), 2.5, ((0, 16), (1, 32))),
        "dblocks": draw_dblocks(jax.random.fold_in(splits[8], 71), 0),
        "dense_tiles": bell_draw(splits[2], (N, N), 1.0, 6.0, ((0, 16), (1, 32))),
        "left_factor": bell_draw(splits[3], (NT, K, N), K ** -0.5, 0.75, ((0, 32), (2, 16))),
        "right_factor": bell_draw(splits[4], (NT, K, N), 1.0, 6.0, ((0, 16), (2, 32))),
        "sketch": bell_draw(splits[5], (K, N), B ** -0.5, 0.25, ((1, 32),)),
        "pattern": touch_ends((jax.random.randint(splits[6], (NT, NT), 0, 4) < 3).astype(jnp.int32), jax.random.fold_in(splits[6], 1), 0, 1),
        "colmap": jax.random.permutation(splits[7], NT).astype(jnp.int32),
    }


def reference(panel, dblocks, dense_tiles, left_factor, right_factor, sketch, pattern, colmap):
    order = NT * B
    split_panel = panel.astype(jnp.float32).reshape(NT, B, PT, B)
    scaled = jnp.einsum("tapq,pqr->tapr", split_panel, dblocks.astype(jnp.float32))
    scaled = scaled.reshape(NT, B, PW).astype(jnp.bfloat16)
    flat_scaled = scaled.reshape(order, PW)

    def one_column(col_pos):
        col_pos = col_pos.astype(jnp.int32)
        panel_tile = lax.dynamic_index_in_dim(panel, colmap[col_pos].astype(jnp.int32), 0, keepdims=False)
        start = (col_pos * B).astype(jnp.int32)
        omega_cols = lax.dynamic_slice_in_dim(sketch, start, B, 1)
        low_flags = lax.dynamic_index_in_dim(pattern, col_pos, 1, keepdims=False) == 1
        dense_cols = lax.dynamic_slice_in_dim(dense_tiles, start, B, 1)
        product = lax.dot_general(flat_scaled, panel_tile, (((1,), (1,)), ((), ())), preferred_element_type=jnp.float32)
        updated = (dense_cols.astype(jnp.float32) - product).astype(jnp.bfloat16).reshape(NT, B, B)
        updated = jnp.where(low_flags[:, None, None], jnp.zeros_like(updated), updated).reshape(order, B)
        projected = lax.dot_general(panel_tile, omega_cols, (((0,), (1,)), ((), ())), preferred_element_type=jnp.float32).astype(jnp.bfloat16)
        right_cols = lax.dynamic_slice_in_dim(right_factor, start, B, 2)
        inner_prod = jnp.einsum("ikb,lb->ikl", right_cols.astype(jnp.float32), omega_cols.astype(jnp.float32)).astype(jnp.bfloat16)
        left_bases = lax.dynamic_index_in_dim(left_factor, col_pos, 0, keepdims=False).reshape(K, NT, B)
        first_term = jnp.einsum("ikl,kib->lib", inner_prod.astype(jnp.float32), left_bases.astype(jnp.float32))
        second_term = lax.dot_general(projected, flat_scaled, (((0,), (1,)), ((), ())), preferred_element_type=jnp.float32)
        sketched = (first_term.reshape(K, order) - second_term).astype(jnp.bfloat16).reshape(K, NT, B)
        sketched = jnp.where(low_flags[None, :, None], sketched, jnp.zeros_like(sketched)).reshape(K, order)
        return updated, sketched

    dense_parts, sketch_parts = lax.map(one_column, jnp.arange(NT, dtype=jnp.int32))
    dense_out = dense_parts.transpose(1, 0, 2).reshape(order, order)
    return dense_out, sketch_parts
```

```python
import jax
import jax.numpy as jnp
from jax import lax
from jax.experimental import pallas as pl
from jax.experimental.pallas import tpu as pltpu
from jax.sharding import PartitionSpec as P

CORES = 2
LANES = 128
HALF = 8


def z_shift(z_count, up, down):
    return [
        (z * CORES + core, (z + (up if core == 0 else down)) % z_count * CORES + core)
        for z in range(z_count)
        for core in range(CORES)
    ]


def core_swap(z_count):
    return [(i, i ^ 1) for i in range(z_count * CORES)]


def same_core(z_count):
    return [[z * CORES + core for z in range(z_count)] for core in range(CORES)]


def same_chip(z_count):
    return [[z * CORES + core for core in range(CORES)] for z in range(z_count)]


def chunk_offsets(z_count):
    offsets = [0]
    step = z_count // 2
    while step >= 1:
        offsets = offsets + [o + step for o in offsets]
        step //= 2
    return offsets


def select_kernel(colmap_ref, tiles_ref, out_ref):
    for j in range(out_ref.shape[0]):
        out_ref[j] = tiles_ref[colmap_ref[j]]


def select_tiles(tiles, colmap):
    return pl.pallas_call(
        select_kernel,
        out_shape=jax.ShapeDtypeStruct(tiles.shape, tiles.dtype),
        in_specs=[
            pl.BlockSpec(memory_space=pltpu.SMEM),
            pl.BlockSpec(memory_space=pltpu.VMEM),
        ],
        out_specs=pl.BlockSpec(memory_space=pltpu.VMEM),
        name="select_tiles",
    )(colmap, tiles)


def final_kernel(
    offsets, info_ref, own_ref, other_ref, right_ref, first_ref, tiles_ref, dense_ref, sketch_ref, rows_ref
):
    z_count = len(offsets)
    piece = own_ref.shape[2]
    slots = own_ref.shape[1]
    tile_size = z_count * CORES * piece
    z_index = info_ref[0]
    core = info_ref[1]
    for from_other, chunk_ref in ((0, own_ref), (1, other_ref)):
        owner = core ^ from_other if from_other else core
        sign = 2 * owner - 1
        for j, offset in enumerate(offsets):
            z_from = (z_index + sign * offset + z_count) & (z_count - 1)
            start = (z_from * CORES + owner) * piece
            for slot in range(slots):
                row = pl.multiple_of(slot * tile_size + start, piece)
                rows_ref[pl.ds(row, piece), :] = chunk_ref[j, slot]
    step = 256
    width = dense_ref.shape[1]

    def body(i, carry):
        row = pl.multiple_of(i * step, step)
        low = info_ref[2 + i // (tile_size // step)] == 1
        product = lax.dot_general(
            rows_ref[pl.ds(row, step), :],
            right_ref[...],
            (((1,), (1,)), ((), ())),
            preferred_element_type=jnp.float32,
        )
        updated = tiles_ref[pl.ds(row, step), :].astype(jnp.float32) - product[:, :width]
        dense_ref[pl.ds(row, step), :] = jnp.where(low, 0.0, updated).astype(dense_ref.dtype)
        sketched = first_ref[:, pl.ds(row, step)] - product[:, width:].T
        sketch_ref[:, pl.ds(row, step)] = jnp.where(low, sketched, 0.0).astype(sketch_ref.dtype)
        return carry

    lax.fori_loop(0, slots * tile_size // step, body, 0)


def final_update(info, own, other, right, first_term, dense_tiles, rank_width):
    z_count, slots, piece, depth = own.shape
    rows = z_count * CORES * slots * piece
    vmem = pl.BlockSpec(memory_space=pltpu.VMEM)

    def kernel(*refs):
        final_kernel(chunk_offsets(z_count), *refs)

    return pl.pallas_call(
        kernel,
        out_shape=(
            jax.ShapeDtypeStruct(dense_tiles.shape, dense_tiles.dtype),
            jax.ShapeDtypeStruct((rank_width, rows), dense_tiles.dtype),
        ),
        in_specs=[pl.BlockSpec(memory_space=pltpu.SMEM)] + [vmem] * 5,
        out_specs=(vmem, vmem),
        scratch_shapes=[pltpu.VMEM((rows, depth), own.dtype)],
        compiler_params=pltpu.CompilerParams(vmem_limit_bytes=40 * 1024 * 1024),
        cost_estimate=pl.CostEstimate(
            flops=2 * rows * depth * right.shape[0], bytes_accessed=8 * 1024 * 1024, transcendentals=0
        ),
        name="final_update",
    )(info, own, other, right, first_term, dense_tiles)


def on_device(panel, dblocks, dense_tiles, left_factor, right_factor, sketch, pattern, colmap):
    slots, piece, depth = panel.shape
    blocks, tile_size, _ = dblocks.shape
    rank_width = sketch.shape[0]
    col_count = tile_size // piece
    z_count = col_count // CORES
    row_count = pattern.shape[0] // slots
    col_index = lax.axis_index("col")
    row_index = lax.axis_index("row")
    z_index = col_index // CORES
    core = col_index % CORES

    scaled = jnp.einsum(
        "sapq,pqr->sapr",
        panel.reshape(slots, piece, blocks, tile_size),
        dblocks,
        preferred_element_type=jnp.float32,
    )
    own = scaled.reshape(1, slots, piece, depth).astype(jnp.bfloat16)
    step = z_count // 2
    while step >= 1:
        own = jnp.concatenate([own, lax.ppermute(own, "col", z_shift(z_count, step, -step))], axis=0)
        step //= 2
    other = lax.ppermute(own, "col", core_swap(z_count))

    lane_blocks = depth // LANES
    halves = piece // HALF
    parts = panel.reshape(slots, halves, HALF, lane_blocks, LANES).transpose(1, 3, 0, 2, 4)
    parts = parts.reshape(row_count, slots, HALF, LANES)
    parts = lax.all_to_all(parts, "row", 0, 0)
    parts = select_tiles(parts.reshape(row_count * slots, HALF, LANES), colmap)
    parts = parts.reshape(z_count, CORES, HALF, LANES)
    parts = lax.all_to_all(parts, "col", 0, 0, axis_index_groups=same_core(z_count))
    parts = lax.all_gather(parts, "col", axis=1, axis_index_groups=same_chip(z_count))
    parts = lax.dynamic_index_in_dim(parts, core, 2, keepdims=False)
    parts = parts.reshape(1, col_count, HALF, LANES)
    parts = jnp.broadcast_to(parts, (row_count, col_count, HALF, LANES))
    parts = lax.all_to_all(parts, "row", 0, 0)
    parts = parts.reshape(halves, lane_blocks, col_count, HALF, LANES).transpose(2, 0, 3, 1, 4)
    column_rows = parts.reshape(tile_size, depth)

    projected = lax.dot_general(
        sketch, column_rows, (((1,), (0,)), ((), ())), preferred_element_type=jnp.float32
    ).astype(jnp.bfloat16)
    right = jnp.concatenate([column_rows, projected], axis=0)

    inner_prod = jnp.einsum(
        "ikb,lb->ikl", right_factor, sketch, preferred_element_type=jnp.float32
    ).astype(jnp.bfloat16)
    left_bases = left_factor[0].reshape(rank_width, slots, tile_size)
    first_term = jnp.einsum(
        "ikl,kib->lib", inner_prod, left_bases, preferred_element_type=jnp.float32
    ).reshape(rank_width, slots * tile_size)

    pattern_col = lax.dynamic_index_in_dim(pattern, col_index, 1, keepdims=False)
    local_flags = lax.dynamic_slice_in_dim(pattern_col, row_index * slots, slots)
    info = jnp.concatenate([jnp.stack([z_index, core]), local_flags]).astype(jnp.int32)
    dense_out, sketch_out = final_update(
        info, own, other, right, first_term, dense_tiles, rank_width
    )
    return dense_out, sketch_out.reshape(1, rank_width, slots * tile_size)


def solution(mesh):
    in_specs = (
        P("row", "col", None),
        P(),
        P("row", "col"),
        P("col", None, "row"),
        P("row", None, "col"),
        P(None, "col"),
        P(),
        P(),
    )
    out_specs = (P("row", "col"), P("col", None, "row"))
    return jax.shard_map(
        on_device, mesh=mesh, in_specs=in_specs, out_specs=out_specs, check_vma=False
    )
```

```python
import jax
import jax.numpy as jnp
from jax import lax
from jax.experimental import pallas as pl
from jax.experimental.pallas import tpu as pltpu
from jax.sharding import PartitionSpec as P

CORES = 2
LANES = 128
HALF = 8
ROW_STEP = 512
VMEM = pl.BlockSpec(memory_space=pltpu.VMEM)
SMEM = pl.BlockSpec(memory_space=pltpu.SMEM)
ANY = pl.BlockSpec(memory_space=pl.ANY)


def z_shift(z_count, up, down):
    return [
        (z * CORES + core, (z + (up if core == 0 else down)) % z_count * CORES + core)
        for z in range(z_count)
        for core in range(CORES)
    ]


def core_swap(z_count):
    return [(i, i ^ 1) for i in range(z_count * CORES)]


def same_core(z_count):
    return [[z * CORES + core for z in range(z_count)] for core in range(CORES)]


def same_chip(z_count):
    return [[z * CORES + core for core in range(CORES)] for z in range(z_count)]


def shift(array, z_count, up, down):
    return lax.ppermute(array, "col", z_shift(z_count, up, down))


def chunk_offsets(z_count):
    half, quarter = z_count // 2, z_count // 4
    return [
        (near[0] + far[0], near[1] + far[1])
        for near in ((0, 0), (-1, 0), (1, 0), (0, 2))
        for far in ((0, 0), (half, 0), (0, quarter), (half, quarter))
    ]


def stack_kernel(*refs):
    *chunk_refs, _, out_ref = refs
    count = chunk_refs[0].shape[0]
    for j, chunk_ref in enumerate(chunk_refs):
        out_ref[j * count : (j + 1) * count] = chunk_ref[...]


def stack_after(chunks, earlier):
    shape = (len(chunks) * chunks[0].shape[0],) + chunks[0].shape[1:]
    return pl.pallas_call(
        stack_kernel,
        out_shape=jax.ShapeDtypeStruct(shape, chunks[0].dtype),
        in_specs=[VMEM] * (len(chunks) + 1),
        out_specs=VMEM,
        compiler_params=pltpu.CompilerParams(vmem_limit_bytes=2 * 1024 * 1024),
        name="stack_after",
    )(*chunks, earlier)


def same_kernel(*refs):
    pass


def hold(array, *earlier):
    return pl.pallas_call(
        same_kernel,
        out_shape=jax.ShapeDtypeStruct(array.shape, array.dtype),
        in_specs=[VMEM] * (1 + len(earlier)),
        out_specs=VMEM,
        input_output_aliases={0: 0},
        compiler_params=pltpu.CompilerParams(vmem_limit_bytes=1024 * 1024),
        name="hold",
    )(array, *earlier)


def select_kernel(colmap_ref, tiles_ref, _, out_ref):
    for j in range(out_ref.shape[0]):
        out_ref[j] = tiles_ref[colmap_ref[j]]


def select_tiles(tiles, colmap, earlier):
    return pl.pallas_call(
        select_kernel,
        out_shape=jax.ShapeDtypeStruct(tiles.shape, tiles.dtype),
        in_specs=[SMEM, VMEM, VMEM],
        out_specs=VMEM,
        compiler_params=pltpu.CompilerParams(vmem_limit_bytes=1024 * 1024),
        name="select_tiles",
    )(colmap, tiles, earlier)


def order_kernel(offsets, info_ref, own_ref, other_ref, rows_ref):
    z_count = len(offsets)
    _, slots, piece, _ = own_ref.shape
    tile_size = z_count * CORES * piece
    z_index = info_ref[0]
    core = info_ref[1]
    for owner, chunk_ref in ((core, own_ref), (1 - core, other_ref)):
        sign = 2 * owner - 1
        for j, (fixed, mirrored) in enumerate(offsets):
            z_from = (z_index + fixed + sign * mirrored + z_count) & (z_count - 1)
            start = (z_from * CORES + owner) * piece
            for slot in range(slots):
                row = pl.multiple_of(slot * tile_size + start, piece)
                rows_ref[pl.ds(row, piece), :] = chunk_ref[j, slot]


def order_rows(info, own, other):
    z_count, slots, piece, depth = own.shape

    def kernel(*refs):
        order_kernel(chunk_offsets(z_count), *refs)

    return pl.pallas_call(
        kernel,
        out_shape=jax.ShapeDtypeStruct((CORES * z_count * slots * piece, depth), own.dtype),
        in_specs=[SMEM, VMEM, VMEM],
        out_specs=VMEM,
        compiler_params=pltpu.CompilerParams(vmem_limit_bytes=6 * 1024 * 1024),
        name="order_rows",
    )(info, own, other)


def final_kernel(
    info_ref, rows_ref, right_ref, first_ref, tiles_ref, dense_ref, sketched_ref
):
    i = pl.program_id(0)
    tile_size = dense_ref.shape[1]
    low = info_ref[2 + i * rows_ref.shape[0] // tile_size] == 1
    product = lax.dot_general(
        rows_ref[...],
        right_ref[...],
        (((1,), (1,)), ((), ())),
        preferred_element_type=jnp.float32,
    )
    updated = tiles_ref[...].astype(jnp.float32) - product[:, :tile_size]
    dense_ref[...] = jnp.where(low, 0.0, updated).astype(dense_ref.dtype)
    sketched = first_ref[...] - product[:, tile_size:].T
    sketched_ref[...] = jnp.where(low, sketched, 0.0).astype(sketched_ref.dtype)


def final_update(info, rows, right, first_term, dense_tiles):
    count, depth = rows.shape
    rank_width, tile_size = first_term.shape[0], dense_tiles.shape[1]
    return pl.pallas_call(
        final_kernel,
        grid=(count // ROW_STEP,),
        out_shape=(
            jax.ShapeDtypeStruct(dense_tiles.shape, dense_tiles.dtype),
            jax.ShapeDtypeStruct((rank_width, count), dense_tiles.dtype),
        ),
        in_specs=[
            SMEM,
            pl.BlockSpec((ROW_STEP, depth), lambda i: (i, 0)),
            VMEM,
            pl.BlockSpec((rank_width, ROW_STEP), lambda i: (0, i)),
            pl.BlockSpec((ROW_STEP, tile_size), lambda i: (i, 0)),
        ],
        out_specs=(
            pl.BlockSpec((ROW_STEP, tile_size), lambda i: (i, 0)),
            pl.BlockSpec((rank_width, ROW_STEP), lambda i: (0, i)),
        ),
        compiler_params=pltpu.CompilerParams(vmem_limit_bytes=12 * 1024 * 1024),
        cost_estimate=pl.CostEstimate(
            flops=2 * count * depth * (tile_size + rank_width),
            bytes_accessed=6 * 1024 * 1024,
            transcendentals=0,
        ),
        name="final_update",
    )(info, rows, right, first_term, dense_tiles)


def on_device(panel, dblocks, dense_tiles, left_factor, right_factor, sketch, pattern, colmap):
    slots, piece, depth = panel.shape
    blocks, tile_size, _ = dblocks.shape
    rank_width = sketch.shape[0]
    col_count = tile_size // piece
    z_count = col_count // CORES
    row_count = pattern.shape[0] // slots
    col_index = lax.axis_index("col")
    row_index = lax.axis_index("row")
    z_index = col_index // CORES
    core = col_index % CORES

    lane_blocks = depth // LANES
    halves = piece // HALF
    parts = panel.reshape(slots, halves, HALF, lane_blocks, LANES).transpose(1, 3, 0, 2, 4)
    parts = parts.reshape(row_count, slots, HALF, LANES)
    parts = lax.all_to_all(parts, "row", 0, 0)
    parts = parts.reshape(row_count * slots, HALF, LANES)

    scaled = jnp.einsum(
        "sapq,pqr->sapr",
        panel.reshape(slots, piece, blocks, tile_size),
        dblocks,
        preferred_element_type=jnp.float32,
    )
    own = scaled.reshape(1, slots, piece, depth).astype(jnp.bfloat16)
    half = shift(own, z_count, z_count // 2, z_count // 2)
    parts = select_tiles(parts, colmap, half)
    own = jnp.concatenate([own, half], axis=0)
    quarter = shift(own, z_count, z_count // 4, -(z_count // 4))
    parts = parts.reshape(z_count, CORES, HALF, LANES)
    parts = lax.all_to_all(parts, "col", 0, 0, axis_index_groups=same_core(z_count))
    own = stack_after([own, quarter], parts)
    parts = lax.all_gather(parts, "col", axis=1, axis_index_groups=same_chip(z_count))
    parts = hold(parts, own)
    parts = lax.dynamic_index_in_dim(parts, core, 2, keepdims=False)
    parts = parts.reshape(1, col_count, HALF, LANES)
    parts = jnp.broadcast_to(parts, (row_count, col_count, HALF, LANES))

    near = [shift(own, z_count, up, down) for up, down in ((1, 1), (-1, -1), (2, -2))]
    own = jnp.concatenate([own] + near, axis=0)

    parts = lax.all_to_all(parts, "row", 0, 0)
    inner_prod = jnp.einsum(
        "ikb,lb->ikl", right_factor, sketch, preferred_element_type=jnp.float32
    ).astype(jnp.bfloat16)
    left_bases = left_factor[0].reshape(rank_width, slots, tile_size)
    first_term = jnp.einsum(
        "ikl,kib->lib", inner_prod, left_bases, preferred_element_type=jnp.float32
    ).reshape(rank_width, slots * tile_size)

    own = hold(own, parts, first_term)
    other = lax.ppermute(own, "col", core_swap(z_count))
    parts = parts.reshape(halves, lane_blocks, col_count, HALF, LANES).transpose(2, 0, 3, 1, 4)
    column_rows = parts.reshape(tile_size, depth)
    projected = lax.dot_general(
        sketch, column_rows, (((1,), (0,)), ((), ())), preferred_element_type=jnp.float32
    ).astype(jnp.bfloat16)
    right = jnp.concatenate([column_rows, projected], axis=0)

    pattern_col = lax.dynamic_index_in_dim(pattern, col_index, 1, keepdims=False)
    local_flags = lax.dynamic_slice_in_dim(pattern_col, row_index * slots, slots)
    info = jnp.concatenate([jnp.stack([z_index, core]), local_flags]).astype(jnp.int32)
    rows = order_rows(info, own, other)
    dense_out, sketch_out = final_update(info, rows, right, first_term, dense_tiles)
    return dense_out, sketch_out.reshape(1, rank_width, slots * tile_size)


def solution(mesh):
    in_specs = (
        P("row", "col", None),
        P(),
        P("row", "col"),
        P("col", None, "row"),
        P("row", None, "col"),
        P(None, "col"),
        P(),
        P(),
    )
    out_specs = (P("row", "col"), P("col", None, "row"))
    return jax.shard_map(
        on_device, mesh=mesh, in_specs=in_specs, out_specs=out_specs, check_vma=False
    )
```

```python
import jax
import jax.numpy as jnp
from jax import lax
from jax.experimental import pallas as pl
from jax.experimental.pallas import tpu as pltpu
from jax.sharding import PartitionSpec as P

CORES = 2
LANES = 128
HALF = 8
ROW_STEP = 512
VMEM = pl.BlockSpec(memory_space=pltpu.VMEM)
SMEM = pl.BlockSpec(memory_space=pltpu.SMEM)
ANY = pl.BlockSpec(memory_space=pl.ANY)


def z_shift(z_count, up, down):
    return [
        (z * CORES + core, (z + (up if core == 0 else down)) % z_count * CORES + core)
        for z in range(z_count)
        for core in range(CORES)
    ]


def core_swap(z_count):
    return [(i, i ^ 1) for i in range(z_count * CORES)]


def same_core(z_count):
    return [[z * CORES + core for z in range(z_count)] for core in range(CORES)]


def same_chip(z_count):
    return [[z * CORES + core for core in range(CORES)] for z in range(z_count)]


def shift(array, z_count, up, down):
    return lax.ppermute(array, "col", z_shift(z_count, up, down))


def far_offsets(z_count):
    half, quarter = z_count // 2, z_count // 4
    return ((0, 0), (half, 0), (0, quarter), (half, quarter))


NEAR_OFFSETS = ((0, 0), (-1, 0), (1, 0), (0, 2))


def stack_kernel(*refs):
    *chunk_refs, _, out_ref = refs
    count = chunk_refs[0].shape[0]
    for j, chunk_ref in enumerate(chunk_refs):
        out_ref[j * count : (j + 1) * count] = chunk_ref[...]


def stack_after(chunks, earlier):
    shape = (len(chunks) * chunks[0].shape[0],) + chunks[0].shape[1:]
    return pl.pallas_call(
        stack_kernel,
        out_shape=jax.ShapeDtypeStruct(shape, chunks[0].dtype),
        in_specs=[VMEM] * (len(chunks) + 1),
        out_specs=VMEM,
        compiler_params=pltpu.CompilerParams(vmem_limit_bytes=2 * 1024 * 1024),
        name="stack_after",
    )(*chunks, earlier)


def same_kernel(*refs):
    pass


def hold(array, *earlier):
    return pl.pallas_call(
        same_kernel,
        out_shape=jax.ShapeDtypeStruct(array.shape, array.dtype),
        in_specs=[VMEM] * (1 + len(earlier)),
        out_specs=VMEM,
        input_output_aliases={0: 0},
        compiler_params=pltpu.CompilerParams(vmem_limit_bytes=1024 * 1024),
        name="hold",
    )(array, *earlier)


def low_rank_kernel(left_ref, right_ref, sketch_ref, _, out_ref):
    slots, _, tile_size = right_ref.shape
    for slot in range(slots):
        columns = slice(slot * tile_size, (slot + 1) * tile_size)
        inner = lax.dot_general(
            sketch_ref[...], right_ref[slot], (((1,), (1,)), ((), ())), preferred_element_type=jnp.float32
        ).astype(left_ref.dtype)
        out_ref[:, columns] = jnp.dot(inner, left_ref[:, columns], preferred_element_type=jnp.float32)


def low_rank_term(left, right, sketch, earlier):
    return pl.pallas_call(
        low_rank_kernel,
        out_shape=jax.ShapeDtypeStruct(left.shape, jnp.float32),
        in_specs=[VMEM, VMEM, VMEM, ANY],
        out_specs=VMEM,
        compiler_params=pltpu.CompilerParams(vmem_limit_bytes=2 * 1024 * 1024),
        name="low_rank_term",
    )(left, right, sketch, earlier)


def select_kernel(colmap_ref, tiles_ref, _, out_ref):
    for j in range(out_ref.shape[0]):
        out_ref[j] = tiles_ref[colmap_ref[j]]


def select_tiles(tiles, colmap, earlier):
    return pl.pallas_call(
        select_kernel,
        out_shape=jax.ShapeDtypeStruct(tiles.shape, tiles.dtype),
        in_specs=[SMEM, VMEM, VMEM],
        out_specs=VMEM,
        compiler_params=pltpu.CompilerParams(vmem_limit_bytes=1024 * 1024),
        name="select_tiles",
    )(colmap, tiles, earlier)


def place(z_index, owner, near, chunk_ref, rows_ref):
    per_piece, slots, piece, _ = chunk_ref.shape
    z_count = rows_ref.shape[0] // (slots * piece * CORES)
    sign = 2 * owner - 1
    for j, far in enumerate(far_offsets(z_count)):
        fixed, mirrored = near[0] + far[0], near[1] + far[1]
        z_from = (z_index + fixed + sign * mirrored + z_count) & (z_count - 1)
        start = (z_from * CORES + owner) * piece
        for slot in range(slots):
            row = pl.multiple_of(slot * z_count * CORES * piece + start, piece)
            rows_ref[pl.ds(row, piece), :] = chunk_ref[j, slot]


def position():
    col_index = lax.axis_index("col")
    return col_index // CORES, col_index % CORES


def order_kernel(*refs):
    *chunk_refs, rows_ref = refs
    z_index, core = position()
    for near, chunk_ref in zip(NEAR_OFFSETS, chunk_refs[:4]):
        place(z_index, core, near, chunk_ref, rows_ref)
    for near, chunk_ref in zip(NEAR_OFFSETS, chunk_refs[4:]):
        place(z_index, 1 - core, near, chunk_ref, rows_ref)


def order_rows(own, other):
    per_piece, slots, piece, depth = own[0].shape
    count = len(own) * per_piece * CORES * slots * piece
    return pl.pallas_call(
        order_kernel,
        out_shape=jax.ShapeDtypeStruct((count, depth), own[0].dtype),
        in_specs=[VMEM] * (len(own) + len(other)),
        out_specs=VMEM,
        compiler_params=pltpu.CompilerParams(vmem_limit_bytes=6 * 1024 * 1024),
        name="order_rows",
    )(*own, *other)


def final_kernel(
    pattern_ref, _, last_ref, right_ref, first_ref, tiles_ref, dense_ref, sketched_ref, rows_ref
):
    i = pl.program_id(0)
    tile_size = dense_ref.shape[1]
    slots = rows_ref.shape[0] // tile_size
    z_index, core = position()

    @pl.when(i == 0)
    def _():
        place(z_index, 1 - core, NEAR_OFFSETS[-1], last_ref, rows_ref)

    tile_row = lax.axis_index("row") * slots + i * ROW_STEP // tile_size
    low = pattern_ref[tile_row, lax.axis_index("col")] == 1
    product = lax.dot_general(
        rows_ref[pl.ds(pl.multiple_of(i * ROW_STEP, ROW_STEP), ROW_STEP), :],
        right_ref[...],
        (((1,), (1,)), ((), ())),
        preferred_element_type=jnp.float32,
    )
    updated = tiles_ref[...].astype(jnp.float32) - product[:, :tile_size]
    dense_ref[...] = jnp.where(low, 0.0, updated).astype(dense_ref.dtype)
    sketched = first_ref[...] - product[:, tile_size:].T
    sketched_ref[...] = jnp.where(low, sketched, 0.0).astype(sketched_ref.dtype)


def final_update(pattern, rows, last, right, first_term, dense_tiles):
    count, depth = rows.shape
    rank_width, tile_size = first_term.shape[0], dense_tiles.shape[1]
    return pl.pallas_call(
        final_kernel,
        grid=(count // ROW_STEP,),
        out_shape=(
            jax.ShapeDtypeStruct(dense_tiles.shape, dense_tiles.dtype),
            jax.ShapeDtypeStruct((rank_width, count), dense_tiles.dtype),
            jax.ShapeDtypeStruct(rows.shape, rows.dtype),
        ),
        in_specs=[
            SMEM,
            VMEM,
            VMEM,
            VMEM,
            pl.BlockSpec((rank_width, ROW_STEP), lambda i: (0, i)),
            pl.BlockSpec((ROW_STEP, tile_size), lambda i: (i, 0)),
        ],
        out_specs=(
            pl.BlockSpec((ROW_STEP, tile_size), lambda i: (i, 0)),
            pl.BlockSpec((rank_width, ROW_STEP), lambda i: (0, i)),
            VMEM,
        ),
        input_output_aliases={1: 2},
        compiler_params=pltpu.CompilerParams(vmem_limit_bytes=12 * 1024 * 1024),
        cost_estimate=pl.CostEstimate(
            flops=2 * count * depth * (tile_size + rank_width),
            bytes_accessed=6 * 1024 * 1024,
            transcendentals=0,
        ),
        name="final_update",
    )(pattern, rows, last, right, first_term, dense_tiles)


def on_device(panel, dblocks, dense_tiles, left_factor, right_factor, sketch, pattern, colmap):
    slots, piece, depth = panel.shape
    blocks, tile_size, _ = dblocks.shape
    rank_width = sketch.shape[0]
    col_count = tile_size // piece
    z_count = col_count // CORES
    row_count = pattern.shape[0] // slots
    col_index = lax.axis_index("col")
    core = col_index % CORES

    lane_blocks = depth // LANES
    halves = piece // HALF
    parts = panel.reshape(slots, halves, HALF, lane_blocks, LANES).transpose(1, 3, 0, 2, 4)
    parts = parts.reshape(row_count, slots, HALF, LANES)
    parts = lax.all_to_all(parts, "row", 0, 0)
    parts = parts.reshape(row_count * slots, HALF, LANES)

    scaled = jnp.einsum(
        "sapq,pqr->sapr",
        panel.reshape(slots, piece, blocks, tile_size),
        dblocks,
        preferred_element_type=jnp.float32,
    )
    own = scaled.reshape(1, slots, piece, depth).astype(jnp.bfloat16)
    half = shift(own, z_count, z_count // 2, z_count // 2)
    parts = select_tiles(parts, colmap, half)
    first_term = low_rank_term(left_factor[0], right_factor, sketch, parts)
    own = jnp.concatenate([own, half], axis=0)
    quarter = shift(own, z_count, z_count // 4, -(z_count // 4))
    parts = parts.reshape(z_count, CORES, HALF, LANES)
    parts = lax.all_to_all(parts, "col", 0, 0, axis_index_groups=same_core(z_count))
    own = stack_after([own, quarter], parts)
    parts = lax.all_gather(parts, "col", axis=1, axis_index_groups=same_chip(z_count))
    parts = hold(parts, own, first_term)
    parts = lax.dynamic_index_in_dim(parts, core, 2, keepdims=False)
    parts = parts.reshape(1, col_count, HALF, LANES)
    parts = jnp.broadcast_to(parts, (row_count, col_count, HALF, LANES))

    own = [own] + [shift(own, z_count, up, down) for up, down in ((1, 1), (-1, -1), (2, -2))]
    other = [lax.ppermute(part, "col", core_swap(z_count)) for part in own[:-1]]

    parts = lax.all_to_all(parts, "row", 0, 0)
    own[-1] = hold(own[-1], parts)
    last = lax.ppermute(own[-1], "col", core_swap(z_count))
    parts = parts.reshape(halves, lane_blocks, col_count, HALF, LANES).transpose(2, 0, 3, 1, 4)
    column_rows = parts.reshape(tile_size, depth)
    projected = lax.dot_general(
        sketch, column_rows, (((1,), (0,)), ((), ())), preferred_element_type=jnp.float32
    ).astype(jnp.bfloat16)
    right = jnp.concatenate([column_rows, projected], axis=0)

    rows = order_rows(own, other)
    dense_out, sketch_out, _ = final_update(pattern, rows, last, right, first_term, dense_tiles)
    return dense_out, sketch_out.reshape(1, rank_width, slots * tile_size)


def solution(mesh):
    in_specs = (
        P("row", "col", None),
        P(),
        P("row", "col"),
        P("col", None, "row"),
        P("row", None, "col"),
        P(None, "col"),
        P(),
        P(),
    )
    out_specs = (P("row", "col"), P("col", None, "row"))
    return jax.shard_map(
        on_device, mesh=mesh, in_specs=in_specs, out_specs=out_specs, check_vma=False
    )
```

```python
import jax
import jax.numpy as jnp
from jax import lax
from jax.experimental import pallas as pl
from jax.experimental.pallas import tpu as pltpu
from jax.sharding import PartitionSpec as P

CORES = 2
LANES = 128
HALF = 8
ROW_STEP = 512
VMEM = pl.BlockSpec(memory_space=pltpu.VMEM)
SMEM = pl.BlockSpec(memory_space=pltpu.SMEM)
ANY = pl.BlockSpec(memory_space=pl.ANY)


def z_shift(z_count, up, down):
    return [
        (z * CORES + core, (z + (up if core == 0 else down)) % z_count * CORES + core)
        for z in range(z_count)
        for core in range(CORES)
    ]


def core_swap(z_count):
    return [(i, i ^ 1) for i in range(z_count * CORES)]


def same_core(z_count):
    return [[z * CORES + core for z in range(z_count)] for core in range(CORES)]


def same_chip(z_count):
    return [[z * CORES + core for core in range(CORES)] for z in range(z_count)]


def shift(array, z_count, up, down):
    return lax.ppermute(array, "col", z_shift(z_count, up, down))


def far_offsets(z_count):
    half, quarter = z_count // 2, z_count // 4
    return ((0, 0), (half, 0), (0, quarter), (half, quarter))


NEAR_OFFSETS = (((0, 0),), ((-1, 0),), ((1, 0), (0, 2)))


def stack_kernel(*refs):
    *chunk_refs, _, out_ref = refs
    count = chunk_refs[0].shape[0]
    for j, chunk_ref in enumerate(chunk_refs):
        out_ref[j * count : (j + 1) * count] = chunk_ref[...]


def stack_after(chunks, earlier):
    shape = (len(chunks) * chunks[0].shape[0],) + chunks[0].shape[1:]
    return pl.pallas_call(
        stack_kernel,
        out_shape=jax.ShapeDtypeStruct(shape, chunks[0].dtype),
        in_specs=[VMEM] * (len(chunks) + 1),
        out_specs=VMEM,
        compiler_params=pltpu.CompilerParams(vmem_limit_bytes=2 * 1024 * 1024),
        name="stack_after",
    )(*chunks, earlier)


def same_kernel(array_ref, *refs):
    refs[-1][...] = array_ref[...]


def hold(array, *earlier):
    return pl.pallas_call(
        same_kernel,
        out_shape=jax.ShapeDtypeStruct(array.shape, array.dtype),
        in_specs=[VMEM] * (1 + len(earlier)),
        out_specs=VMEM,
        input_output_aliases={0: 0},
        compiler_params=pltpu.CompilerParams(vmem_limit_bytes=4 * 1024 * 1024),
        name="hold",
    )(array, *earlier)


def low_rank_kernel(left_ref, right_ref, sketch_ref, _, out_ref):
    slots, _, tile_size = right_ref.shape
    for slot in range(slots):
        columns = slice(slot * tile_size, (slot + 1) * tile_size)
        inner = lax.dot_general(
            sketch_ref[...], right_ref[slot], (((1,), (1,)), ((), ())), preferred_element_type=jnp.float32
        ).astype(left_ref.dtype)
        out_ref[:, columns] = jnp.dot(inner, left_ref[:, columns], preferred_element_type=jnp.float32)


def low_rank_term(left, right, sketch, earlier):
    return pl.pallas_call(
        low_rank_kernel,
        out_shape=jax.ShapeDtypeStruct(left.shape, jnp.float32),
        in_specs=[VMEM, VMEM, VMEM, ANY],
        out_specs=VMEM,
        compiler_params=pltpu.CompilerParams(vmem_limit_bytes=2 * 1024 * 1024),
        name="low_rank_term",
    )(left, right, sketch, earlier)


def select_kernel(colmap_ref, tiles_ref, _, out_ref):
    for j in range(out_ref.shape[0]):
        out_ref[j] = tiles_ref[colmap_ref[j]]


def select_tiles(tiles, colmap, earlier):
    return pl.pallas_call(
        select_kernel,
        out_shape=jax.ShapeDtypeStruct(tiles.shape, tiles.dtype),
        in_specs=[SMEM, VMEM, VMEM],
        out_specs=VMEM,
        compiler_params=pltpu.CompilerParams(vmem_limit_bytes=1024 * 1024),
        name="select_tiles",
    )(colmap, tiles, earlier)


def place(z_index, owner, nears, chunk_ref, rows_ref):
    _, slots, piece, _ = chunk_ref.shape
    z_count = rows_ref.shape[0] // (slots * piece * CORES)
    sign = 2 * owner - 1
    offsets = [(near, far) for near in nears for far in far_offsets(z_count)]
    for j, (near, far) in enumerate(offsets):
        fixed, mirrored = near[0] + far[0], near[1] + far[1]
        z_from = (z_index + fixed + sign * mirrored + z_count) & (z_count - 1)
        start = (z_from * CORES + owner) * piece
        for slot in range(slots):
            row = pl.multiple_of(slot * z_count * CORES * piece + start, piece)
            rows_ref[pl.ds(row, piece), :] = chunk_ref[j, slot]


def position():
    col_index = lax.axis_index("col")
    return col_index // CORES, col_index % CORES


def order_kernel(*refs):
    *chunk_refs, rows_ref = refs
    z_index, core = position()
    for near, chunk_ref in zip(NEAR_OFFSETS, chunk_refs[: len(NEAR_OFFSETS)]):
        place(z_index, core, near, chunk_ref, rows_ref)
    for near, chunk_ref in zip(NEAR_OFFSETS, chunk_refs[len(NEAR_OFFSETS) :]):
        place(z_index, 1 - core, near, chunk_ref, rows_ref)


def order_rows(own, other):
    _, slots, piece, depth = own[0].shape
    count = sum(part.shape[0] for part in own) * CORES * slots * piece
    return pl.pallas_call(
        order_kernel,
        out_shape=jax.ShapeDtypeStruct((count, depth), own[0].dtype),
        in_specs=[VMEM] * (len(own) + len(other)),
        out_specs=VMEM,
        compiler_params=pltpu.CompilerParams(vmem_limit_bytes=6 * 1024 * 1024),
        name="order_rows",
    )(*own, *other)


def final_kernel(
    pattern_ref, rows_ref, last_ref, right_ref, first_ref, tiles_ref, dense_ref, sketched_ref, _
):
    i = pl.program_id(0)
    tile_size = dense_ref.shape[1]
    slots = rows_ref.shape[0] // tile_size
    z_index, core = position()

    @pl.when(i == 0)
    def _():
        place(z_index, 1 - core, NEAR_OFFSETS[-1], last_ref, rows_ref)

    tile_row = lax.axis_index("row") * slots + i * ROW_STEP // tile_size
    low = pattern_ref[tile_row, lax.axis_index("col")] == 1
    product = lax.dot_general(
        rows_ref[pl.ds(pl.multiple_of(i * ROW_STEP, ROW_STEP), ROW_STEP), :],
        right_ref[...],
        (((1,), (1,)), ((), ())),
        preferred_element_type=jnp.float32,
    )
    updated = tiles_ref[...].astype(jnp.float32) - product[:, :tile_size]
    dense_ref[...] = jnp.where(low, 0.0, updated).astype(dense_ref.dtype)
    sketched = first_ref[...] - product[:, tile_size:].T
    sketched_ref[...] = jnp.where(low, sketched, 0.0).astype(sketched_ref.dtype)


def final_update(pattern, rows, last, right, first_term, dense_tiles):
    count, depth = rows.shape
    rank_width, tile_size = first_term.shape[0], dense_tiles.shape[1]
    return pl.pallas_call(
        final_kernel,
        grid=(count // ROW_STEP,),
        out_shape=(
            jax.ShapeDtypeStruct(dense_tiles.shape, dense_tiles.dtype),
            jax.ShapeDtypeStruct((rank_width, count), dense_tiles.dtype),
            jax.ShapeDtypeStruct(rows.shape, rows.dtype),
        ),
        in_specs=[
            SMEM,
            VMEM,
            VMEM,
            VMEM,
            pl.BlockSpec((rank_width, ROW_STEP), lambda i: (0, i)),
            pl.BlockSpec((ROW_STEP, tile_size), lambda i: (i, 0)),
        ],
        out_specs=(
            pl.BlockSpec((ROW_STEP, tile_size), lambda i: (i, 0)),
            pl.BlockSpec((rank_width, ROW_STEP), lambda i: (0, i)),
            VMEM,
        ),
        input_output_aliases={1: 2},
        compiler_params=pltpu.CompilerParams(vmem_limit_bytes=12 * 1024 * 1024),
        cost_estimate=pl.CostEstimate(
            flops=2 * count * depth * (tile_size + rank_width),
            bytes_accessed=6 * 1024 * 1024,
            transcendentals=0,
        ),
        name="final_update",
    )(pattern, rows, last, right, first_term, dense_tiles)


def on_device(panel, dblocks, dense_tiles, left_factor, right_factor, sketch, pattern, colmap):
    slots, piece, depth = panel.shape
    blocks, tile_size, _ = dblocks.shape
    rank_width = sketch.shape[0]
    col_count = tile_size // piece
    z_count = col_count // CORES
    row_count = pattern.shape[0] // slots
    col_index = lax.axis_index("col")
    core = col_index % CORES

    lane_blocks = depth // LANES
    halves = piece // HALF
    parts = panel.reshape(slots, halves, HALF, lane_blocks, LANES).transpose(1, 3, 0, 2, 4)
    parts = parts.reshape(row_count, slots, HALF, LANES)
    parts = lax.all_to_all(parts, "row", 0, 0)
    parts = parts.reshape(row_count * slots, HALF, LANES)

    scaled = jnp.einsum(
        "sapq,pqr->sapr",
        panel.reshape(slots, piece, blocks, tile_size),
        dblocks,
        preferred_element_type=jnp.float32,
    )
    own = scaled.reshape(1, slots, piece, depth).astype(jnp.bfloat16)
    half = shift(own, z_count, z_count // 2, z_count // 2)
    parts = select_tiles(parts, colmap, half)
    first_term = low_rank_term(left_factor[0], right_factor, sketch, parts)
    own = jnp.concatenate([own, half], axis=0)
    quarter = shift(own, z_count, z_count // 4, -(z_count // 4))
    parts = parts.reshape(z_count, CORES, HALF, LANES)
    parts = lax.all_to_all(parts, "col", 0, 0, axis_index_groups=same_core(z_count))
    own = stack_after([own, quarter], parts)
    parts = lax.all_gather(parts, "col", axis=1, axis_index_groups=same_chip(z_count))
    parts = hold(parts, own, first_term)
    parts = lax.dynamic_index_in_dim(parts, core, 2, keepdims=False)
    parts = parts.reshape(1, col_count, HALF, LANES)
    parts = jnp.broadcast_to(parts, (row_count, col_count, HALF, LANES))

    near = [shift(own, z_count, up, down) for up, down in ((1, 1), (-1, -1), (2, -2))]
    own = [own, near[0]]
    other = [lax.ppermute(part, "col", core_swap(z_count)) for part in own]

    parts = lax.all_to_all(parts, "row", 0, 0)
    own.append(hold(jnp.concatenate(near[1:], axis=0), parts))
    last = lax.ppermute(own[-1], "col", core_swap(z_count))
    parts = parts.reshape(halves, lane_blocks, col_count, HALF, LANES).transpose(2, 0, 3, 1, 4)
    column_rows = parts.reshape(tile_size, depth)
    projected = lax.dot_general(
        sketch, column_rows, (((1,), (0,)), ((), ())), preferred_element_type=jnp.float32
    ).astype(jnp.bfloat16)
    right = jnp.concatenate([column_rows, projected], axis=0)

    rows = order_rows(own, other)
    dense_out, sketch_out, _ = final_update(pattern, rows, last, right, first_term, dense_tiles)
    return dense_out, sketch_out.reshape(1, rank_width, slots * tile_size)


def solution(mesh):
    in_specs = (
        P("row", "col", None),
        P(),
        P("row", "col"),
        P("col", None, "row"),
        P("row", None, "col"),
        P(None, "col"),
        P(),
        P(),
    )
    out_specs = (P("row", "col"), P("col", None, "row"))
    return jax.shard_map(
        on_device, mesh=mesh, in_specs=in_specs, out_specs=out_specs, check_vma=False
    )
```

```python
import jax
import jax.numpy as jnp
from jax import lax
from jax.experimental import pallas as pl
from jax.experimental.pallas import tpu as pltpu
from jax.sharding import PartitionSpec as P

CORES = 2
LANES = 128
HALF = 8
ROW_STEP = 512
VMEM = pl.BlockSpec(memory_space=pltpu.VMEM)
SMEM = pl.BlockSpec(memory_space=pltpu.SMEM)
ANY = pl.BlockSpec(memory_space=pl.ANY)


def z_shift(z_count, up, down):
    return [
        (z * CORES + core, (z + (up if core == 0 else down)) % z_count * CORES + core)
        for z in range(z_count)
        for core in range(CORES)
    ]


def core_swap(z_count):
    return [(i, i ^ 1) for i in range(z_count * CORES)]


def shift(array, z_count, up, down):
    return lax.ppermute(array, "col", z_shift(z_count, up, down))


def far_offsets(z_count):
    half, quarter = z_count // 2, z_count // 4
    return ((0, 0), (half, 0), (0, quarter), (half, quarter))


NEAR_OFFSETS = (((0, 0),), ((-1, 0),), ((1, 0), (0, 2)))


def stack_kernel(*refs):
    *chunk_refs, _, out_ref = refs
    count = chunk_refs[0].shape[0]
    for j, chunk_ref in enumerate(chunk_refs):
        out_ref[j * count : (j + 1) * count] = chunk_ref[...]


def stack_after(chunks, earlier):
    shape = (len(chunks) * chunks[0].shape[0],) + chunks[0].shape[1:]
    return pl.pallas_call(
        stack_kernel,
        out_shape=jax.ShapeDtypeStruct(shape, chunks[0].dtype),
        in_specs=[VMEM] * (len(chunks) + 1),
        out_specs=VMEM,
        compiler_params=pltpu.CompilerParams(vmem_limit_bytes=2 * 1024 * 1024),
        name="stack_after",
    )(*chunks, earlier)


def same_kernel(array_ref, *refs):
    refs[-1][...] = array_ref[...]


def hold(array, *earlier):
    return pl.pallas_call(
        same_kernel,
        out_shape=jax.ShapeDtypeStruct(array.shape, array.dtype),
        in_specs=[VMEM] * (1 + len(earlier)),
        out_specs=VMEM,
        input_output_aliases={0: 0},
        compiler_params=pltpu.CompilerParams(vmem_limit_bytes=4 * 1024 * 1024),
        name="hold",
    )(array, *earlier)


def low_rank_kernel(left_ref, right_ref, sketch_ref, _, out_ref):
    slots, _, tile_size = right_ref.shape
    for slot in range(slots):
        columns = slice(slot * tile_size, (slot + 1) * tile_size)
        inner = lax.dot_general(
            sketch_ref[...], right_ref[slot], (((1,), (1,)), ((), ())), preferred_element_type=jnp.float32
        ).astype(left_ref.dtype)
        out_ref[:, columns] = jnp.dot(inner, left_ref[:, columns], preferred_element_type=jnp.float32)


def low_rank_term(left, right, sketch, earlier):
    return pl.pallas_call(
        low_rank_kernel,
        out_shape=jax.ShapeDtypeStruct(left.shape, jnp.float32),
        in_specs=[VMEM, VMEM, VMEM, ANY],
        out_specs=VMEM,
        compiler_params=pltpu.CompilerParams(vmem_limit_bytes=2 * 1024 * 1024),
        name="low_rank_term",
    )(left, right, sketch, earlier)


def select_kernel(colmap_ref, tiles_ref, _, out_ref):
    for j in range(out_ref.shape[0]):
        out_ref[j] = tiles_ref[colmap_ref[j]]


def select_tiles(tiles, colmap, earlier):
    return pl.pallas_call(
        select_kernel,
        out_shape=jax.ShapeDtypeStruct(tiles.shape, tiles.dtype),
        in_specs=[SMEM, VMEM, VMEM],
        out_specs=VMEM,
        compiler_params=pltpu.CompilerParams(vmem_limit_bytes=1024 * 1024),
        name="select_tiles",
    )(colmap, tiles, earlier)


def place(z_index, owner, nears, chunk_ref, rows_ref):
    _, slots, piece, _ = chunk_ref.shape
    z_count = rows_ref.shape[0] // (slots * piece * CORES)
    sign = 2 * owner - 1
    offsets = [(near, far) for near in nears for far in far_offsets(z_count)]
    for j, (near, far) in enumerate(offsets):
        fixed, mirrored = near[0] + far[0], near[1] + far[1]
        z_from = (z_index + fixed + sign * mirrored + z_count) & (z_count - 1)
        start = (z_from * CORES + owner) * piece
        for slot in range(slots):
            row = pl.multiple_of(slot * z_count * CORES * piece + start, piece)
            rows_ref[pl.ds(row, piece), :] = chunk_ref[j, slot]


def position():
    col_index = lax.axis_index("col")
    return col_index // CORES, col_index % CORES


def order_kernel(*refs):
    *chunk_refs, rows_ref = refs
    z_index, core = position()
    for near, chunk_ref in zip(NEAR_OFFSETS, chunk_refs[: len(NEAR_OFFSETS)]):
        place(z_index, core, near, chunk_ref, rows_ref)
    for near, chunk_ref in zip(NEAR_OFFSETS, chunk_refs[len(NEAR_OFFSETS) :]):
        place(z_index, 1 - core, near, chunk_ref, rows_ref)


def order_rows(own, other):
    _, slots, piece, depth = own[0].shape
    count = sum(part.shape[0] for part in own) * CORES * slots * piece
    return pl.pallas_call(
        order_kernel,
        out_shape=jax.ShapeDtypeStruct((count, depth), own[0].dtype),
        in_specs=[VMEM] * (len(own) + len(other)),
        out_specs=VMEM,
        compiler_params=pltpu.CompilerParams(vmem_limit_bytes=6 * 1024 * 1024),
        name="order_rows",
    )(*own, *other)


def final_kernel(
    pattern_ref, rows_ref, last_ref, right_ref, first_ref, tiles_ref, dense_ref, sketched_ref, _
):
    i = pl.program_id(0)
    tile_size = dense_ref.shape[1]
    slots = rows_ref.shape[0] // tile_size
    z_index, core = position()

    @pl.when(i == 0)
    def _():
        place(z_index, 1 - core, NEAR_OFFSETS[-1], last_ref, rows_ref)

    tile_row = lax.axis_index("row") * slots + i * ROW_STEP // tile_size
    low = pattern_ref[tile_row, lax.axis_index("col")] == 1
    product = lax.dot_general(
        rows_ref[pl.ds(pl.multiple_of(i * ROW_STEP, ROW_STEP), ROW_STEP), :],
        right_ref[...],
        (((1,), (1,)), ((), ())),
        preferred_element_type=jnp.float32,
    )
    updated = tiles_ref[...].astype(jnp.float32) - product[:, :tile_size]
    dense_ref[...] = jnp.where(low, 0.0, updated).astype(dense_ref.dtype)
    sketched = first_ref[...] - product[:, tile_size:].T
    sketched_ref[...] = jnp.where(low, sketched, 0.0).astype(sketched_ref.dtype)


def final_update(pattern, rows, last, right, first_term, dense_tiles):
    count, depth = rows.shape
    rank_width, tile_size = first_term.shape[0], dense_tiles.shape[1]
    return pl.pallas_call(
        final_kernel,
        grid=(count // ROW_STEP,),
        out_shape=(
            jax.ShapeDtypeStruct(dense_tiles.shape, dense_tiles.dtype),
            jax.ShapeDtypeStruct((rank_width, count), dense_tiles.dtype),
            jax.ShapeDtypeStruct(rows.shape, rows.dtype),
        ),
        in_specs=[
            SMEM,
            VMEM,
            VMEM,
            VMEM,
            pl.BlockSpec((rank_width, ROW_STEP), lambda i: (0, i)),
            pl.BlockSpec((ROW_STEP, tile_size), lambda i: (i, 0)),
        ],
        out_specs=(
            pl.BlockSpec((ROW_STEP, tile_size), lambda i: (i, 0)),
            pl.BlockSpec((rank_width, ROW_STEP), lambda i: (0, i)),
            VMEM,
        ),
        input_output_aliases={1: 2},
        compiler_params=pltpu.CompilerParams(vmem_limit_bytes=12 * 1024 * 1024),
        cost_estimate=pl.CostEstimate(
            flops=2 * count * depth * (tile_size + rank_width),
            bytes_accessed=6 * 1024 * 1024,
            transcendentals=0,
        ),
        name="final_update",
    )(pattern, rows, last, right, first_term, dense_tiles)


def on_device(panel, dblocks, dense_tiles, left_factor, right_factor, sketch, pattern, colmap):
    slots, piece, depth = panel.shape
    blocks, tile_size, _ = dblocks.shape
    rank_width = sketch.shape[0]
    col_count = tile_size // piece
    z_count = col_count // CORES
    row_count = pattern.shape[0] // slots
    lane_blocks = depth // LANES
    halves = piece // HALF
    parts = panel.reshape(slots, halves, HALF, lane_blocks, LANES).transpose(1, 3, 0, 2, 4)
    parts = parts.reshape(row_count, slots, HALF, LANES)
    parts = lax.all_to_all(parts, "row", 0, 0)
    parts = parts.reshape(row_count * slots, HALF, LANES)

    scaled = jnp.einsum(
        "sapq,pqr->sapr",
        panel.reshape(slots, piece, blocks, tile_size),
        dblocks,
        preferred_element_type=jnp.float32,
    )
    own = scaled.reshape(1, slots, piece, depth).astype(jnp.bfloat16)
    half = shift(own, z_count, z_count // 2, z_count // 2)
    parts = select_tiles(parts, colmap, half)
    first_term = low_rank_term(left_factor[0], right_factor, sketch, parts)
    own = jnp.concatenate([own, half], axis=0)
    quarter = shift(own, z_count, z_count // 4, -(z_count // 4))
    parts = parts.reshape(col_count, HALF, LANES)
    parts = lax.all_to_all(parts, "col", 0, 0)
    own = stack_after([own, quarter], parts)
    parts = hold(parts, own, first_term)
    parts = parts.reshape(1, col_count, HALF, LANES)
    parts = jnp.broadcast_to(parts, (row_count, col_count, HALF, LANES))

    near = [shift(own, z_count, up, down) for up, down in ((1, 1), (-1, -1), (2, -2))]
    own = [own, near[0]]
    other = [lax.ppermute(part, "col", core_swap(z_count)) for part in own]

    parts = lax.all_to_all(parts, "row", 0, 0)
    own.append(hold(jnp.concatenate(near[1:], axis=0), parts))
    last = lax.ppermute(own[-1], "col", core_swap(z_count))
    parts = parts.reshape(halves, lane_blocks, col_count, HALF, LANES).transpose(2, 0, 3, 1, 4)
    column_rows = parts.reshape(tile_size, depth)
    projected = lax.dot_general(
        sketch, column_rows, (((1,), (0,)), ((), ())), preferred_element_type=jnp.float32
    ).astype(jnp.bfloat16)
    right = jnp.concatenate([column_rows, projected], axis=0)

    rows = order_rows(own, other)
    dense_out, sketch_out, _ = final_update(pattern, rows, last, right, first_term, dense_tiles)
    return dense_out, sketch_out.reshape(1, rank_width, slots * tile_size)


def solution(mesh):
    in_specs = (
        P("row", "col", None),
        P(),
        P("row", "col"),
        P("col", None, "row"),
        P("row", None, "col"),
        P(None, "col"),
        P(),
        P(),
    )
    out_specs = (P("row", "col"), P("col", None, "row"))
    return jax.shard_map(
        on_device, mesh=mesh, in_specs=in_specs, out_specs=out_specs, check_vma=False
    )
```

```python
import jax
import jax.numpy as jnp
from jax import lax
from jax.experimental import pallas as pl
from jax.experimental.pallas import tpu as pltpu
from jax.sharding import PartitionSpec as P

CORES = 2
LANES = 128
HALF = 8
ROW_STEP = 512
VMEM = pl.BlockSpec(memory_space=pltpu.VMEM)
SMEM = pl.BlockSpec(memory_space=pltpu.SMEM)
ANY = pl.BlockSpec(memory_space=pl.ANY)


def z_shift(z_count, up, down):
    return [
        (z * CORES + core, (z + (up if core == 0 else down)) % z_count * CORES + core)
        for z in range(z_count)
        for core in range(CORES)
    ]


def core_swap(z_count):
    return [(i, i ^ 1) for i in range(z_count * CORES)]


def shift(array, z_count, up, down):
    return lax.ppermute(array, "col", z_shift(z_count, up, down))


def far_offsets(z_count):
    half, quarter = z_count // 2, z_count // 4
    return ((0, 0), (half, 0), (0, quarter), (half, quarter))


NEAR_OFFSETS = (((0, 0),), ((-1, 0),), ((1, 0), (0, 2)))


def stack_kernel(*refs):
    *chunk_refs, _, out_ref = refs
    count = chunk_refs[0].shape[0]
    for j, chunk_ref in enumerate(chunk_refs):
        out_ref[j * count : (j + 1) * count] = chunk_ref[...]


def stack_after(chunks, earlier):
    shape = (len(chunks) * chunks[0].shape[0],) + chunks[0].shape[1:]
    return pl.pallas_call(
        stack_kernel,
        out_shape=jax.ShapeDtypeStruct(shape, chunks[0].dtype),
        in_specs=[VMEM] * (len(chunks) + 1),
        out_specs=VMEM,
        compiler_params=pltpu.CompilerParams(vmem_limit_bytes=2 * 1024 * 1024),
        name="stack_after",
    )(*chunks, earlier)


def same_kernel(array_ref, *refs):
    refs[-1][...] = array_ref[...]


def hold(array, *earlier):
    return pl.pallas_call(
        same_kernel,
        out_shape=jax.ShapeDtypeStruct(array.shape, array.dtype),
        in_specs=[VMEM] * (1 + len(earlier)),
        out_specs=VMEM,
        input_output_aliases={0: 0},
        compiler_params=pltpu.CompilerParams(vmem_limit_bytes=4 * 1024 * 1024),
        name="hold",
    )(array, *earlier)


def spread_kernel(parts_ref, *refs):
    out_ref = refs[-1]
    part = parts_ref[...]
    for row in range(out_ref.shape[0]):
        out_ref[row] = part


def spread(parts, row_count, *earlier):
    return pl.pallas_call(
        spread_kernel,
        out_shape=jax.ShapeDtypeStruct((row_count,) + parts.shape, parts.dtype),
        in_specs=[VMEM] * (1 + len(earlier)),
        out_specs=VMEM,
        compiler_params=pltpu.CompilerParams(vmem_limit_bytes=4 * 1024 * 1024),
        name="spread",
    )(parts, *earlier)


def low_rank_kernel(left_ref, right_ref, sketch_ref, _, out_ref):
    slots, _, tile_size = right_ref.shape
    for slot in range(slots):
        columns = slice(slot * tile_size, (slot + 1) * tile_size)
        inner = lax.dot_general(
            sketch_ref[...], right_ref[slot], (((1,), (1,)), ((), ())), preferred_element_type=jnp.float32
        ).astype(left_ref.dtype)
        out_ref[:, columns] = jnp.dot(inner, left_ref[:, columns], preferred_element_type=jnp.float32)


def low_rank_term(left, right, sketch, earlier):
    return pl.pallas_call(
        low_rank_kernel,
        out_shape=jax.ShapeDtypeStruct(left.shape, jnp.float32),
        in_specs=[VMEM, VMEM, VMEM, ANY],
        out_specs=VMEM,
        compiler_params=pltpu.CompilerParams(vmem_limit_bytes=2 * 1024 * 1024),
        name="low_rank_term",
    )(left, right, sketch, earlier)


def select_kernel(colmap_ref, tiles_ref, _, out_ref):
    for j in range(out_ref.shape[0]):
        out_ref[j] = tiles_ref[colmap_ref[j]]


def select_tiles(tiles, colmap, earlier):
    return pl.pallas_call(
        select_kernel,
        out_shape=jax.ShapeDtypeStruct(tiles.shape, tiles.dtype),
        in_specs=[SMEM, VMEM, VMEM],
        out_specs=VMEM,
        compiler_params=pltpu.CompilerParams(vmem_limit_bytes=1024 * 1024),
        name="select_tiles",
    )(colmap, tiles, earlier)


def place(z_index, owner, nears, chunk_ref, rows_ref):
    _, slots, piece, _ = chunk_ref.shape
    z_count = rows_ref.shape[0] // (slots * piece * CORES)
    sign = 2 * owner - 1
    offsets = [(near, far) for near in nears for far in far_offsets(z_count)]
    for j, (near, far) in enumerate(offsets):
        fixed, mirrored = near[0] + far[0], near[1] + far[1]
        z_from = (z_index + fixed + sign * mirrored + z_count) & (z_count - 1)
        start = (z_from * CORES + owner) * piece
        for slot in range(slots):
            row = pl.multiple_of(slot * z_count * CORES * piece + start, piece)
            rows_ref[pl.ds(row, piece), :] = chunk_ref[j, slot]


def position():
    col_index = lax.axis_index("col")
    return col_index // CORES, col_index % CORES


def order_kernel(*refs):
    *chunk_refs, rows_ref = refs
    z_index, core = position()
    for near, chunk_ref in zip(NEAR_OFFSETS, chunk_refs[: len(NEAR_OFFSETS)]):
        place(z_index, core, near, chunk_ref, rows_ref)
    for near, chunk_ref in zip(NEAR_OFFSETS, chunk_refs[len(NEAR_OFFSETS) :]):
        place(z_index, 1 - core, near, chunk_ref, rows_ref)


def order_rows(own, other):
    _, slots, piece, depth = own[0].shape
    count = sum(part.shape[0] for part in own) * CORES * slots * piece
    return pl.pallas_call(
        order_kernel,
        out_shape=jax.ShapeDtypeStruct((count, depth), own[0].dtype),
        in_specs=[VMEM] * (len(own) + len(other)),
        out_specs=VMEM,
        compiler_params=pltpu.CompilerParams(vmem_limit_bytes=6 * 1024 * 1024),
        name="order_rows",
    )(*own, *other)


def final_kernel(
    pattern_ref, rows_ref, last_ref, right_ref, first_ref, tiles_ref, dense_ref, sketched_ref, _
):
    i = pl.program_id(0)
    tile_size = dense_ref.shape[1]
    slots = rows_ref.shape[0] // tile_size
    z_index, core = position()

    @pl.when(i == 0)
    def _():
        place(z_index, 1 - core, NEAR_OFFSETS[-1], last_ref, rows_ref)

    tile_row = lax.axis_index("row") * slots + i * ROW_STEP // tile_size
    low = pattern_ref[tile_row, lax.axis_index("col")] == 1
    product = lax.dot_general(
        rows_ref[pl.ds(pl.multiple_of(i * ROW_STEP, ROW_STEP), ROW_STEP), :],
        right_ref[...],
        (((1,), (1,)), ((), ())),
        preferred_element_type=jnp.float32,
    )
    updated = tiles_ref[...].astype(jnp.float32) - product[:, :tile_size]
    dense_ref[...] = jnp.where(low, 0.0, updated).astype(dense_ref.dtype)
    sketched = first_ref[...] - product[:, tile_size:].T
    sketched_ref[...] = jnp.where(low, sketched, 0.0).astype(sketched_ref.dtype)


def final_update(pattern, rows, last, right, first_term, dense_tiles):
    count, depth = rows.shape
    rank_width, tile_size = first_term.shape[0], dense_tiles.shape[1]
    return pl.pallas_call(
        final_kernel,
        grid=(count // ROW_STEP,),
        out_shape=(
            jax.ShapeDtypeStruct(dense_tiles.shape, dense_tiles.dtype),
            jax.ShapeDtypeStruct((rank_width, count), dense_tiles.dtype),
            jax.ShapeDtypeStruct(rows.shape, rows.dtype),
        ),
        in_specs=[
            SMEM,
            VMEM,
            VMEM,
            VMEM,
            pl.BlockSpec((rank_width, ROW_STEP), lambda i: (0, i)),
            pl.BlockSpec((ROW_STEP, tile_size), lambda i: (i, 0)),
        ],
        out_specs=(
            pl.BlockSpec((ROW_STEP, tile_size), lambda i: (i, 0)),
            pl.BlockSpec((rank_width, ROW_STEP), lambda i: (0, i)),
            VMEM,
        ),
        input_output_aliases={1: 2},
        compiler_params=pltpu.CompilerParams(vmem_limit_bytes=12 * 1024 * 1024),
        cost_estimate=pl.CostEstimate(
            flops=2 * count * depth * (tile_size + rank_width),
            bytes_accessed=6 * 1024 * 1024,
            transcendentals=0,
        ),
        name="final_update",
    )(pattern, rows, last, right, first_term, dense_tiles)


def on_device(panel, dblocks, dense_tiles, left_factor, right_factor, sketch, pattern, colmap):
    slots, piece, depth = panel.shape
    blocks, tile_size, _ = dblocks.shape
    rank_width = sketch.shape[0]
    col_count = tile_size // piece
    z_count = col_count // CORES
    row_count = pattern.shape[0] // slots
    lane_blocks = depth // LANES
    halves = piece // HALF
    parts = panel.reshape(slots, halves, HALF, lane_blocks, LANES).transpose(1, 3, 0, 2, 4)
    parts = parts.reshape(row_count, slots, HALF, LANES)
    parts = lax.all_to_all(parts, "row", 0, 0)
    parts = parts.reshape(row_count * slots, HALF, LANES)

    scaled = jnp.einsum(
        "sapq,pqr->sapr",
        panel.reshape(slots, piece, blocks, tile_size),
        dblocks,
        preferred_element_type=jnp.float32,
    )
    own = scaled.reshape(1, slots, piece, depth).astype(jnp.bfloat16)
    half = shift(own, z_count, z_count // 2, z_count // 2)
    parts = select_tiles(parts, colmap, half)
    first_term = low_rank_term(left_factor[0], right_factor, sketch, parts)
    own = jnp.concatenate([own, half], axis=0)
    quarter = shift(own, z_count, z_count // 4, -(z_count // 4))
    parts = parts.reshape(col_count, HALF, LANES)
    parts = lax.all_to_all(parts, "col", 0, 0)
    own = stack_after([own, quarter], parts)
    parts = spread(parts, row_count, own, first_term)

    near = [shift(own, z_count, up, down) for up, down in ((1, 1), (-1, -1), (2, -2))]
    own = [own, near[0]]
    other = [lax.ppermute(part, "col", core_swap(z_count)) for part in own]

    parts = lax.all_to_all(parts, "row", 0, 0)
    own.append(hold(jnp.concatenate(near[1:], axis=0), parts))
    last = lax.ppermute(own[-1], "col", core_swap(z_count))
    parts = parts.reshape(halves, lane_blocks, col_count, HALF, LANES).transpose(2, 0, 3, 1, 4)
    column_rows = parts.reshape(tile_size, depth)
    projected = lax.dot_general(
        sketch, column_rows, (((1,), (0,)), ((), ())), preferred_element_type=jnp.float32
    ).astype(jnp.bfloat16)
    right = jnp.concatenate([column_rows, projected], axis=0)

    rows = order_rows(own, other)
    dense_out, sketch_out, _ = final_update(pattern, rows, last, right, first_term, dense_tiles)
    return dense_out, sketch_out.reshape(1, rank_width, slots * tile_size)


def solution(mesh):
    in_specs = (
        P("row", "col", None),
        P(),
        P("row", "col"),
        P("col", None, "row"),
        P("row", None, "col"),
        P(None, "col"),
        P(),
        P(),
    )
    out_specs = (P("row", "col"), P("col", None, "row"))
    return jax.shard_map(
        on_device, mesh=mesh, in_specs=in_specs, out_specs=out_specs, check_vma=False
    )
```
